512 devices in a mesh: pp: 8 (over y, z_hi), ep: 64 (over x, z_lo, core).
Axes of the slice: x: 4, y: 4, z: 16 (z_hi: 2, z_lo: 8; z = z_hi * 8 + z_lo), core: 2. Of those that a mesh axis runs over, the one named last changes fastest.
Arguments:
- carried: bfloat16 [8, 4096, 3584], P('pp', 'ep'), may hold values from -6 to 6
- saved: bfloat16 [8, 4096, 3584], P('pp', 'ep'), may hold values from -6 to 6
- grads_prev: bfloat16 [8, 4096, 3584], P('pp', 'ep'), may hold values from -6 to 6
- routes_fwd: int32 [8, 4096, 1], P('pp', 'ep'), may hold values from 0 to 7; in each aligned block of 64 rows (0 to 63, 64 to 127, ..., all dimensions but the last counted through in order) at most 8 rows name the same one
- gates_fwd: float32 [8, 4096, 1], P('pp', 'ep'), may hold values from 0.1 to 1
- routes_bwd: int32 [8, 4096, 1], P('pp', 'ep'), may hold values from 0 to 7; in each aligned block of 64 rows (0 to 63, 64 to 127, ..., all dimensions but the last counted through in order) at most 8 rows name the same one
- gates_bwd: float32 [8, 4096, 1], P('pp', 'ep'), may hold values from 0.1 to 1
- w_gate: bfloat16 [8, 64, 3584, 128], P('pp', 'ep'), may hold values from -0.09375 to 0.09375
- w_up: bfloat16 [8, 64, 3584, 128], P('pp', 'ep'), may hold values from -0.09375 to 0.09375
- w_down: bfloat16 [8, 64, 128, 3584], P('pp', 'ep'), may hold values from -0.1875 to 0.1875
Outputs:
- acts: bfloat16 [8, 4096, 3584], P('pp', 'ep')
- input_grads: bfloat16 [8, 4096, 3584], P('pp', 'ep')
The draws below stay inside these ranges and needn't reach their ends.
Inputs may be any that keep to these rules, and one draw needn't show every extreme that they name: `routes_fwd`: in the rows of one device every expert is named by exactly 8 routes. `routes_bwd`: in the rows of one device every expert is named by exactly 8 routes.
All inputs are finite; a program needn't handle non-finite values.
Results may differ from the reference program's by a relative error of at most 0.01.
Values may be sent and summed in bfloat16 or wider, within the bound.
No kernel may reach another device: no remote copies, remote signals or barrier semaphores. Data moves between devices by JAX's collectives and lax.ppermute only.
A program may use at most 64 MiB of HBM per device.

```python
import math
import jax
import jax.numpy as jnp
import numpy as np
from jax import lax

D = 3584
FFE = 1024
W = 8
TOP = 1
TOK_F = 64
TOK_B = 64
EXPERTS = 8
FFE_DEV = 128
TOKENS_F = 4096
TOKENS_B = 4096
CAP_F = 8
CAP_B = 8
N_PP = 8
N_EP = 64


def shard_levels(own_key, shape, split, low, largest):
    gain, own = 1.0, jax.random.fold_in(own_key, 6)
    for position, shards_of in split:
        steps = jnp.exp(jax.random.uniform(jax.random.fold_in(own, position), (shards_of,), jnp.float32, low / len(split), largest / len(split)))
        gain = gain * jnp.repeat(steps, shape[position] // shards_of).reshape([-1 if axis == position else 1 for axis in range(len(shape))])
    return gain


def shared_out(own_key, own, number, rows, number_of, top, reach, slope):
    ranking = jax.random.permutation(own_key, number_of)
    crowded, ordinary = load_shares(number_of, rows * top, reach, slope, True), load_shares(number_of, rows * top, reach, slope, False)
    places = jnp.arange(number_of)

    def named(sizes, turn):
        used = int((sizes > 0).sum())
        fixed = max(1, used // 4)
        shifted = fixed + (places - fixed + turn * (used - fixed)) % max(1, number_of - fixed)
        return jnp.zeros((number_of,), jnp.int32).at[ranking[jnp.where(places < fixed, places, shifted)]].set(jnp.asarray(sizes, jnp.int32))

    sizes = jnp.where(number % 4 == 0, named(crowded, number // 4), named(ordinary, number - number // 4 - 1))
    mixed = jax.random.permutation(jax.random.fold_in(own, 3), number_of)
    donor, receiver = mixed[0:number_of // 2 * 2:2], mixed[1:number_of // 2 * 2:2]
    room = jnp.minimum(sizes[donor] - 1, reach - sizes[receiver]) // 2
    room = jnp.where((donor == ranking[0]) | (receiver == ranking[0]) | (sizes[receiver] == 0), 0, jnp.maximum(room, 0))
    shifted = jax.random.randint(jax.random.fold_in(own, 4), (number_of // 2,), 0, 1 << 20) % (room + 1)
    sizes = sizes.at[donor].add(-shifted).at[receiver].add(shifted)
    items = jnp.searchsorted(jnp.cumsum(sizes), jnp.arange(rows * top), side="right").astype(jnp.int32)
    listing = items.reshape(top, rows).T
    listing = listing[jax.random.permutation(jax.random.fold_in(own, 1), rows)]
    turn = jax.random.randint(jax.random.fold_in(own, 2), (rows, 1), 0, top)
    return jnp.take_along_axis(listing, (jnp.arange(top)[None, :] + turn) % top, axis=1)


def load_shares(count, total, most, skew, full):
    loads = [(1 << 20) // math.isqrt(grade ** skew) + 1 for grade in range(1, count + 1)]
    largest = most if full else min(most, max(-(-total // count), total * loads[0] // sum(loads)))
    least = 1 if total - largest >= count - 1 else 0
    counts, surplus = [largest] + [least] * (count - 1), total - largest - least * (count - 1)
    while surplus > 0:
        candidates = [i for i in range(1, count) if counts[i] < largest] or [i for i in range(1, count) if counts[i] < most]
        mass, left = sum([loads[i] for i in candidates]), surplus
        for i in candidates:
            extra = min(most - counts[i], max(1, left * loads[i] // mass), surplus)
            counts[i] = counts[i] + extra
            surplus = surplus - extra
    return np.array(counts)


def gaussian(key, dims, spread, bound, cuts=(), kind=jnp.bfloat16):
    values = spread * jax.random.normal(key, dims, jnp.float32)
    if cuts:
        values = values * shard_levels(key, dims, cuts, -0.22, 0.18)
    return jnp.clip(values, -bound, bound).astype(kind)


def setup_inputs(seed: int = 0) -> dict:
    key_list = jax.random.split(jax.random.key(seed), 11)
    carried = gaussian(key_list[0], (N_PP, TOKENS_F, D), 1.0, 6.0, ((0, 8), (1, 64)))
    saved = gaussian(key_list[1], (N_PP, TOKENS_B, D), 1.0, 6.0, ((0, 8), (1, 64)))
    grads_prev = gaussian(key_list[2], (N_PP, TOKENS_B, D), 1.0, 6.0, ((0, 8), (1, 64)))
    routes_fwd_keys = jax.random.split(jax.random.fold_in(key_list[3], 1), N_PP * TOKENS_F // TOK_F)
    routes_fwd_turns = jax.random.permutation(jax.random.fold_in(key_list[3], 3), N_PP * TOKENS_F // TOK_F)
    routes_fwd = jax.vmap(lambda own, number: shared_out(jax.random.fold_in(key_list[3], 2), own, number, TOK_F, EXPERTS, TOP, CAP_F, 0))(routes_fwd_keys, routes_fwd_turns).reshape((N_PP, TOKENS_F, TOP))
    gates_fwd = jnp.clip(0.1 + 0.9 * jax.random.uniform(key_list[4], (N_PP, TOKENS_F, TOP), jnp.float32) ** shard_levels(key_list[4], (N_PP, TOKENS_F, TOP), ((0, 8), (1, 64)), -0.2, 0.2), 0.1, 1.0)
    routes_bwd_keys = jax.random.split(jax.random.fold_in(key_list[5], 1), N_PP * TOKENS_B // TOK_B)
    routes_bwd_turns = jax.random.permutation(jax.random.fold_in(key_list[5], 3), N_PP * TOKENS_B // TOK_B)
    routes_bwd = jax.vmap(lambda own, number: shared_out(jax.random.fold_in(key_list[5], 2), own, number, TOK_B, EXPERTS, TOP, CAP_B, 0))(routes_bwd_keys, routes_bwd_turns).reshape((N_PP, TOKENS_B, TOP))
    gates_bwd = jnp.clip(0.1 + 0.9 * jax.random.uniform(key_list[6], (N_PP, TOKENS_B, TOP), jnp.float32) ** shard_levels(key_list[6], (N_PP, TOKENS_B, TOP), ((0, 8), (1, 64)), -0.2, 0.2), 0.1, 1.0)
    w_gate = gaussian(key_list[7], (N_PP, N_EP, D, FFE_DEV), D ** -0.5, 0.09375, ((0, 8), (1, 64)))
    w_up = gaussian(key_list[8], (N_PP, N_EP, D, FFE_DEV), D ** -0.5, 0.09375, ((0, 8), (1, 64)))
    w_down = gaussian(key_list[9], (N_PP, N_EP, FFE_DEV, D), FFE ** -0.5, 0.1875, ((0, 8), (1, 64)))
    return {"carried": carried, "saved": saved, "grads_prev": grads_prev, "routes_fwd": routes_fwd, "gates_fwd": gates_fwd, "routes_bwd": routes_bwd, "gates_bwd": gates_bwd, "w_gate": w_gate, "w_up": w_up, "w_down": w_down}


epsilon = 1e-06

def normalize(activations):
    values = activations.astype(jnp.float32)
    rms_scale = lax.rsqrt(lax.optimization_barrier(jnp.mean(values * values, axis=-1, keepdims=True)) + epsilon)
    return (values * rms_scale, rms_scale)

def slot_positions(routes, slot_depth):
    flat_routes = routes.reshape(-1).astype(jnp.int32)
    onehot = (flat_routes[:, None] == jnp.arange(EXPERTS, dtype=jnp.int32)[None, :]).astype(jnp.int32)
    ranked = jnp.cumsum(onehot, axis=0) - 1
    return (flat_routes * slot_depth + lax.optimization_barrier(jnp.sum(ranked * onehot, axis=1))).astype(jnp.int32)

def pack_rows(token_rows, slot_index, count):
    return jnp.zeros((count, token_rows.shape[1]), token_rows.dtype).at[slot_index].set(token_rows)

def expert_out(packed):
    expert_rows, gate_weights, up_weights, down_weights = packed
    rows_wide = expert_rows.astype(jnp.float32)
    gate_pre = jnp.einsum('rd,wdf->wrf', rows_wide, gate_weights.astype(jnp.float32))
    up_pre = jnp.einsum('rd,wdf->wrf', rows_wide, up_weights.astype(jnp.float32))
    hidden = (jax.nn.silu(gate_pre) * up_pre).astype(jnp.bfloat16)
    parts = jnp.einsum('wrf,wfd->wrd', hidden.astype(jnp.float32), down_weights.astype(jnp.float32)).astype(jnp.bfloat16)
    return lax.optimization_barrier(jnp.sum(parts.astype(jnp.float32), axis=0))

def expert_grad(packed):
    expert_rows, cotangents, gate_weights, up_weights, down_weights = packed
    rows_wide = expert_rows.astype(jnp.float32)
    gate_wide = gate_weights.astype(jnp.float32)
    up_wide = up_weights.astype(jnp.float32)
    gate_pre = jnp.einsum('rd,wdf->wrf', rows_wide, gate_wide)
    up_pre = jnp.einsum('rd,wdf->wrf', rows_wide, up_wide)
    hidden_grad = jnp.einsum('rd,wfd->wrf', cotangents.astype(jnp.float32), down_weights.astype(jnp.float32))
    sigmoid_val = jax.nn.sigmoid(gate_pre)
    gate_grad = (hidden_grad * up_pre * sigmoid_val * (1.0 + gate_pre * (1.0 - sigmoid_val))).astype(jnp.bfloat16)
    up_grad = (hidden_grad * jax.nn.silu(gate_pre)).astype(jnp.bfloat16)
    parts = jnp.einsum('wrf,wdf->wrd', gate_grad.astype(jnp.float32), gate_wide) + jnp.einsum('wrf,wdf->wrd', up_grad.astype(jnp.float32), up_wide)
    return lax.optimization_barrier(jnp.sum(parts.astype(jnp.bfloat16).astype(jnp.float32), axis=0))

def section_forward(section_input, routes, gates, gate_weights, up_weights, down_weights):
    slot_depth = N_EP * CAP_F
    normed, rms_scale = normalize(section_input)
    slots = slot_positions(routes, slot_depth)
    token_rows = jnp.repeat(normed.astype(jnp.bfloat16), TOP, axis=0)
    packed = pack_rows(token_rows, slots, EXPERTS * slot_depth).reshape(EXPERTS, slot_depth, D)
    results = lax.map(expert_out, (packed, gate_weights, up_weights, down_weights))
    picked = results.reshape(EXPERTS * slot_depth, D)[slots].reshape(section_input.shape[0], TOP, D)
    mixture = jnp.einsum('tk,tkd->td', gates.astype(jnp.float32), picked)
    return (section_input.astype(jnp.float32) + mixture).astype(jnp.bfloat16)

def section_backward(section_input, cotangent, routes, gates, gate_weights, up_weights, down_weights):
    slot_depth = N_EP * CAP_B
    normed, rms_scale = normalize(section_input)
    slots = slot_positions(routes, slot_depth)
    token_rows = jnp.repeat(normed.astype(jnp.bfloat16), TOP, axis=0)
    gated = (gates.astype(jnp.float32)[:, :, None] * cotangent.astype(jnp.float32)[:, None, :]).astype(jnp.bfloat16).reshape(-1, D)
    packed = pack_rows(token_rows, slots, EXPERTS * slot_depth).reshape(EXPERTS, slot_depth, D)
    packed_cot = pack_rows(gated, slots, EXPERTS * slot_depth).reshape(EXPERTS, slot_depth, D)
    results = lax.map(expert_grad, (packed, packed_cot, gate_weights, up_weights, down_weights))
    picked = results.reshape(EXPERTS * slot_depth, D)[slots].reshape(section_input.shape[0], TOP, D)
    summed = lax.optimization_barrier(jnp.sum(picked, axis=1))
    projection = lax.optimization_barrier(jnp.mean(normed * summed, axis=-1, keepdims=True))
    return (cotangent.astype(jnp.float32) + rms_scale * (summed - normed * projection)).astype(jnp.bfloat16)

def reference(carried, saved, grads_prev, routes_fwd, gates_fwd, routes_bwd, gates_bwd, w_gate, w_up, w_down):
    outputs = []
    gradients = []
    for section_index in range(N_PP):
        gate_weights = w_gate[section_index].reshape(EXPERTS, W, D, FFE_DEV)
        up_weights = w_up[section_index].reshape(EXPERTS, W, D, FFE_DEV)
        down_weights = w_down[section_index].reshape(EXPERTS, W, FFE_DEV, D)
        section_input = carried[(section_index - 1) % N_PP]
        outputs.append(section_forward(section_input, routes_fwd[section_index], gates_fwd[section_index], gate_weights, up_weights, down_weights))
        cotangent = grads_prev[(section_index + 1) % N_PP]
        gradients.append(section_backward(saved[section_index], cotangent, routes_bwd[section_index], gates_bwd[section_index], gate_weights, up_weights, down_weights))
    return (jnp.stack(outputs), jnp.stack(gradients))
```

```python
import jax
import jax.numpy as jnp
from jax import lax
from jax.sharding import Mesh
from jax.sharding import PartitionSpec as P

AXES = ("y", "zh", "x", "zq", "zr", "c")
SIZES = (4, 2, 4, 2, 4, 2)
PP = ("y", "zh")
EP = ("x", "zq", "zr", "c")
Z16 = ("zh", "zq", "zr")
Z8 = ("zq", "zr")
EXPERTS = 8
DEPTH = 8
ROWS = EXPERTS * DEPTH
LANES = 128


epsilon = 1e-06


def normalize(activations):
    values = activations.astype(jnp.float32)
    rms_scale = lax.rsqrt(jnp.mean(values * values, axis=-1, keepdims=True) + epsilon)
    return (values * rms_scale, rms_scale)


def slot_matrix(routes):
    same = routes[:, None] == routes[None, :]
    order = jnp.arange(ROWS, dtype=jnp.int32)
    earlier = order[None, :] < order[:, None]
    rank = jnp.sum((same & earlier).astype(jnp.int32), axis=1)
    place = (routes % 2) * 4 + routes // 2
    slots = place * DEPTH + rank
    return (order[:, None] == slots[None, :]).astype(jnp.bfloat16)


def reorder(matrix, rows):
    return jnp.dot(matrix, rows, preferred_element_type=jnp.float32).astype(jnp.bfloat16)


def gate_lanes(gates):
    first = gates.astype(jnp.bfloat16)
    left = gates - first.astype(jnp.float32)
    second = left.astype(jnp.bfloat16)
    third = (left - second.astype(jnp.float32)).astype(jnp.bfloat16)
    three = jnp.stack([first, second, third], axis=1)
    return jnp.pad(three, ((0, 0), (0, LANES - 3)))


def gate_of(lanes):
    wide = lanes[:, :3].astype(jnp.float32)
    return (wide[:, 2:3] + wide[:, 1:2]) + wide[:, 0:1]


def rotated(x, axis, by):
    length = lax.axis_size(axis)
    return lax.ppermute(x, axis, [(i, (i + by) % length) for i in range(length)])


def gather_x(rows):
    return [rows] + [rotated(rows, "x", j) for j in (1, 2, 3)]


def scatter_sum_x(parts):
    own = parts[:ROWS]
    sent = parts.astype(jnp.bfloat16)
    total = own.astype(jnp.bfloat16).astype(jnp.float32)
    for j in (1, 2, 3):
        total = total + rotated(sent[j * ROWS : (j + 1) * ROWS], "x", -j).astype(jnp.float32)
    return total


def nt(a, b):
    return lax.dot_general(a, b, (((1,), (1,)), ((), ())), preferred_element_type=jnp.float32)


def expert_out(rows, gate_weights, up_weights, down_weights):
    gate_pre = nt(rows, gate_weights)
    up_pre = nt(rows, up_weights)
    hidden = (jax.nn.silu(gate_pre) * up_pre).astype(jnp.bfloat16)
    return jnp.dot(hidden, down_weights, preferred_element_type=jnp.float32)


def expert_grad(rows, cotangents, gate_weights, up_weights, down_weights):
    gate_pre = nt(rows, gate_weights)
    up_pre = nt(rows, up_weights)
    hidden_grad = nt(cotangents, down_weights)
    sigmoid_val = jax.nn.sigmoid(gate_pre)
    gate_grad = (
        hidden_grad * up_pre * sigmoid_val * (1.0 + gate_pre * (1.0 - sigmoid_val))
    ).astype(jnp.bfloat16)
    up_grad = (hidden_grad * jax.nn.silu(gate_pre)).astype(jnp.bfloat16)
    return jnp.dot(gate_grad, gate_weights, preferred_element_type=jnp.float32) + jnp.dot(
        up_grad, up_weights, preferred_element_type=jnp.float32
    )


def weights_along_x(w_gate, w_up, w_down):
    x, zr = lax.axis_index("x"), lax.axis_index("zr")
    stacked = jnp.stack([w_gate.T, w_up.T, w_down])
    units = stacked.shape[1] // 4
    pieces = stacked.reshape(3, 4, units, stacked.shape[2])

    def piece(index):
        return lax.dynamic_index_in_dim(pieces, index, axis=1, keepdims=False)

    along_x = jnp.stack(
        [piece(x)] + [rotated(piece((x + k) % 4), "x", k) for k in (1, 2, 3)]
    )

    def block(index):
        return lax.dynamic_index_in_dim(along_x, index % 4, axis=0, keepdims=False)

    return [block(x - zr - m + 8) for m in range(4)]


def weights_along_z(blocks):
    return blocks[:1] + [rotated(blocks[m], "zr", m) for m in (1, 2, 3)]


def weights_of_chip(blocks):
    mine = jnp.concatenate(blocks, axis=1)
    other = lax.ppermute(mine, "c", [(0, 1), (1, 0)])
    both = jnp.concatenate([mine, other], axis=1)
    return both[0], both[1], both[2]


def body(
    carried, saved, grads_prev, routes_fwd, gates_fwd, routes_bwd, gates_bwd, w_gate, w_up, w_down
):
    high = lax.axis_index("zh")
    features = carried.shape[2]
    own_fwd, own_bwd = routes_fwd[0, :, 0], routes_bwd[0, :, 0]
    flat = jnp.stack(
        [own_fwd.astype(jnp.float32), gates_fwd[0, :, 0], own_bwd.astype(jnp.float32), gates_bwd[0, :, 0]]
    )
    is_high = high == 1
    along_y = jnp.where(is_high, carried[0], grads_prev[0])
    flat, along_y = lax.optimization_barrier((flat, along_y))
    flat = lax.ppermute(flat, "zh", [(0, 1), (1, 0)])
    mid_fwd, mid_bwd = flat[0].astype(jnp.int32), flat[2].astype(jnp.int32)
    moves = []
    for y in range(4):
        moves.append((y * 2 + 1, ((y + 1) % 4) * 2 + 1))
        moves.append((y * 2, ((y + 3) % 4) * 2))
    along_y = lax.ppermute(along_y, PP, moves)
    fwd_rows = jnp.where(is_high, along_y, carried[0])
    cot_rows = jnp.where(is_high, grads_prev[0], along_y)

    blocks = weights_along_x(w_gate[0, 0], w_up[0, 0], w_down[0, 0])

    def dispatch(own, cross):
        both = jnp.concatenate(
            [jnp.where(is_high, cross, own), jnp.where(is_high, own, cross)], axis=0
        ).reshape(2 * EXPERTS, DEPTH, features + LANES)
        got = lax.all_to_all(both, Z16, split_axis=0, concat_axis=0, tiled=True)
        got = got.reshape(2, ROWS, features + LANES)
        return jnp.where(is_high, got[1], got[0]), jnp.where(is_high, got[0], got[1])

    def give_back(rows):
        got = lax.all_to_all(
            rows.reshape(EXPERTS, DEPTH, features), Z8, split_axis=0, concat_axis=0, tiled=True
        )
        return got.reshape(ROWS, features)

    home_bwd = slot_matrix(own_bwd)
    send_saved = jnp.pad(reorder(home_bwd, saved[0]), ((0, 0), (0, LANES)))
    send_cot = reorder(
        slot_matrix(mid_bwd), jnp.concatenate([cot_rows, gate_lanes(flat[3])], axis=1)
    )
    got_saved, got_cot = dispatch(send_saved, send_cot)
    blocks = weights_along_z(blocks)
    send_fwd = reorder(
        slot_matrix(mid_fwd), jnp.concatenate([fwd_rows, gate_lanes(flat[1])], axis=1)
    )
    send_fwd, blocks = lax.optimization_barrier((send_fwd, blocks))
    _, got_fwd = dispatch(jnp.zeros_like(send_fwd), send_fwd)

    normed_bwd, scale_bwd = normalize(got_saved[:, :features])
    cotangent = got_cot[:, :features].astype(jnp.float32)
    gated = (gate_of(got_cot[:, features:]) * cotangent).astype(jnp.bfloat16)
    gathered = [
        rows.reshape(2, ROWS, features)
        for rows in gather_x(jnp.concatenate([normed_bwd.astype(jnp.bfloat16), gated], axis=0))
    ]
    all_normed = jnp.concatenate([rows[0] for rows in gathered], axis=0)
    all_gated = jnp.concatenate([rows[1] for rows in gathered], axis=0)
    gate_weights, up_weights, down_weights = weights_of_chip(blocks)
    parts = expert_grad(
        all_normed,
        all_gated,
        gate_weights,
        up_weights,
        down_weights,
    )
    summed = scatter_sum_x(parts)
    projection = jnp.mean(normed_bwd * summed, axis=-1, keepdims=True)
    grads = (cotangent + scale_bwd * (summed - normed_bwd * projection)).astype(jnp.bfloat16)
    output_grad = reorder(home_bwd.T, give_back(grads))

    section_input = got_fwd[:, :features]
    normed_fwd, _ = normalize(section_input)
    parts = expert_out(
        jnp.concatenate(gather_x(normed_fwd.astype(jnp.bfloat16)), axis=0),
        gate_weights, up_weights, down_weights
    )
    mixture = gate_of(got_fwd[:, features:]) * scatter_sum_x(parts)
    acts = (section_input.astype(jnp.float32) + mixture).astype(jnp.bfloat16)
    output_act = reorder(slot_matrix(own_fwd).T, give_back(acts))
    return (output_act[None], output_grad[None])


def solution(mesh):
    fine = Mesh(mesh.devices.reshape(SIZES), AXES)
    rows = P(PP, EP, None)
    weights = P(PP, EP, None, None)
    return jax.shard_map(
        body,
        mesh=fine,
        in_specs=(rows,) * 7 + (weights,) * 3,
        out_specs=(rows, rows),
        check_vma=False,
    )
```

```python
import jax
import jax.numpy as jnp
from jax import lax
from jax.sharding import Mesh
from jax.sharding import PartitionSpec as P

AXES = ("y", "zh", "x", "zq", "zr", "c")
SIZES = (4, 2, 4, 2, 4, 2)
PP = ("y", "zh")
EP = ("x", "zq", "zr", "c")
Z16 = ("zh", "zq", "zr")
Z8 = ("zq", "zr")
EXPERTS = 8
DEPTH = 8
ROWS = EXPERTS * DEPTH
LANES = 128


epsilon = 1e-06


def normalize(activations):
    values = activations.astype(jnp.float32)
    rms_scale = lax.rsqrt(jnp.mean(values * values, axis=-1, keepdims=True) + epsilon)
    return (values * rms_scale, rms_scale)


def slot_matrix(routes):
    same = routes[:, None] == routes[None, :]
    order = jnp.arange(ROWS, dtype=jnp.int32)
    earlier = order[None, :] < order[:, None]
    rank = jnp.sum((same & earlier).astype(jnp.int32), axis=1)
    place = (routes % 2) * 4 + routes // 2
    slots = place * DEPTH + rank
    return (order[:, None] == slots[None, :]).astype(jnp.bfloat16)


def reorder(matrix, rows):
    return jnp.dot(matrix, rows, preferred_element_type=jnp.float32).astype(jnp.bfloat16)


def gate_lanes(gates):
    first = gates.astype(jnp.bfloat16)
    left = gates - first.astype(jnp.float32)
    second = left.astype(jnp.bfloat16)
    third = (left - second.astype(jnp.float32)).astype(jnp.bfloat16)
    three = jnp.stack([first, second, third], axis=1)
    return jnp.pad(three, ((0, 0), (0, LANES - 3)))


def gate_of(lanes):
    wide = lanes[:, :3].astype(jnp.float32)
    return (wide[:, 2:3] + wide[:, 1:2]) + wide[:, 0:1]


def rotated(x, axis, by):
    length = lax.axis_size(axis)
    return lax.ppermute(x, axis, [(i, (i + by) % length) for i in range(length)])


def gather_x(rows):
    return jnp.concatenate([rows] + [rotated(rows, "x", j) for j in (1, 2, 3)], axis=0)


def scatter_sum_x(parts):
    own = parts[:ROWS]
    sent = parts.astype(jnp.bfloat16)
    total = own.astype(jnp.bfloat16).astype(jnp.float32)
    for j in (1, 2, 3):
        total = total + rotated(sent[j * ROWS : (j + 1) * ROWS], "x", -j).astype(jnp.float32)
    return total


def nt(a, b):
    return lax.dot_general(a, b, (((1,), (1,)), ((), ())), preferred_element_type=jnp.float32)


def expert_out(rows, gate_weights, up_weights, down_weights):
    gate_pre = nt(rows, gate_weights)
    up_pre = nt(rows, up_weights)
    hidden = (jax.nn.silu(gate_pre) * up_pre).astype(jnp.bfloat16)
    return jnp.dot(hidden, down_weights, preferred_element_type=jnp.float32)


def expert_grad(rows, cotangents, gate_weights, up_weights, down_weights):
    gate_pre = nt(rows, gate_weights)
    up_pre = nt(rows, up_weights)
    hidden_grad = nt(cotangents, down_weights)
    sigmoid_val = jax.nn.sigmoid(gate_pre)
    gate_grad = (
        hidden_grad * up_pre * sigmoid_val * (1.0 + gate_pre * (1.0 - sigmoid_val))
    ).astype(jnp.bfloat16)
    up_grad = (hidden_grad * jax.nn.silu(gate_pre)).astype(jnp.bfloat16)
    return jnp.dot(gate_grad, gate_weights, preferred_element_type=jnp.float32) + jnp.dot(
        up_grad, up_weights, preferred_element_type=jnp.float32
    )


def weights_along_x(w_gate, w_up, w_down):
    x, zr = lax.axis_index("x"), lax.axis_index("zr")
    stacked = jnp.stack([w_gate.T, w_up.T, w_down])
    units = stacked.shape[1] // 4
    pieces = stacked.reshape(3, 4, units, stacked.shape[2])

    def piece(index):
        return lax.dynamic_index_in_dim(pieces, index, axis=1, keepdims=False)

    along_x = jnp.stack(
        [piece(x)] + [rotated(piece((x + k) % 4), "x", k) for k in (1, 2, 3)]
    )

    def block(index):
        return lax.dynamic_index_in_dim(along_x, index % 4, axis=0, keepdims=False)

    return [block(x - zr - m + 8) for m in range(4)]


def weights_along_z(blocks):
    return blocks[:1] + [rotated(blocks[m], "zr", m) for m in (1, 2, 3)]


def weights_of_chip(blocks):
    mine = jnp.concatenate(blocks, axis=1)
    other = lax.ppermute(mine, "c", [(0, 1), (1, 0)])
    both = jnp.concatenate([mine, other], axis=1)
    return both[0], both[1], both[2]


def body(
    carried, saved, grads_prev, routes_fwd, gates_fwd, routes_bwd, gates_bwd, w_gate, w_up, w_down
):
    high = lax.axis_index("zh")
    features = carried.shape[2]
    own_fwd, own_bwd = routes_fwd[0, :, 0], routes_bwd[0, :, 0]
    flat = jnp.stack(
        [own_fwd.astype(jnp.float32), gates_fwd[0, :, 0], own_bwd.astype(jnp.float32), gates_bwd[0, :, 0]]
    )
    is_high = high == 1
    along_y = jnp.where(is_high, carried[0], grads_prev[0])
    moves = []
    for y in range(4):
        moves.append((y * 2 + 1, ((y + 1) % 4) * 2 + 1))
        moves.append((y * 2, ((y + 3) % 4) * 2))
    along_y = lax.ppermute(along_y, PP, moves)
    flat, along_y = lax.optimization_barrier((flat, along_y))
    flat = lax.ppermute(flat, "zh", [(0, 1), (1, 0)])
    mid_fwd, mid_bwd = flat[0].astype(jnp.int32), flat[2].astype(jnp.int32)
    fwd_rows = jnp.where(is_high, along_y, carried[0])
    cot_rows = jnp.where(is_high, grads_prev[0], along_y)

    blocks = weights_along_x(w_gate[0, 0], w_up[0, 0], w_down[0, 0])

    def dispatch(own, cross):
        both = jnp.concatenate(
            [jnp.where(is_high, cross, own), jnp.where(is_high, own, cross)], axis=0
        ).reshape(2 * EXPERTS, DEPTH, features + LANES)
        return lax.all_to_all(both, Z16, split_axis=0, concat_axis=0, tiled=True)

    def sides(got):
        got = got.reshape(2, ROWS, features + LANES)
        return jnp.where(is_high, got[1], got[0]), jnp.where(is_high, got[0], got[1])

    def give_back(rows):
        got = lax.all_to_all(
            rows.reshape(EXPERTS, DEPTH, features), Z8, split_axis=0, concat_axis=0, tiled=True
        )
        return got.reshape(ROWS, features)

    home_bwd = slot_matrix(own_bwd)
    send_saved = jnp.pad(reorder(home_bwd, saved[0]), ((0, 0), (0, LANES)))
    send_fwd = reorder(
        slot_matrix(mid_fwd), jnp.concatenate([fwd_rows, gate_lanes(flat[1])], axis=1)
    )
    got_saved, got_fwd = sides(dispatch(send_saved, send_fwd))
    blocks = weights_along_z(blocks)
    send_cot = reorder(
        slot_matrix(mid_bwd), jnp.concatenate([cot_rows, gate_lanes(flat[3])], axis=1)
    )
    got_cot = dispatch(jnp.zeros_like(send_cot), send_cot)
    gate_weights, up_weights, down_weights = weights_of_chip(blocks)

    section_input = got_fwd[:, :features]
    normed_fwd, _ = normalize(section_input)
    parts = expert_out(
        gather_x(normed_fwd.astype(jnp.bfloat16)), gate_weights, up_weights, down_weights
    )
    normed_bwd, scale_bwd = normalize(got_saved[:, :features])
    all_normed = gather_x(normed_bwd.astype(jnp.bfloat16))
    mixed = scatter_sum_x(parts)
    mixed, all_normed, got_cot = lax.optimization_barrier((mixed, all_normed, got_cot))
    _, got_cot = sides(got_cot)
    mixture = gate_of(got_fwd[:, features:]) * mixed
    acts = (section_input.astype(jnp.float32) + mixture).astype(jnp.bfloat16)
    output_act = reorder(slot_matrix(own_fwd).T, give_back(acts))

    cotangent = got_cot[:, :features].astype(jnp.float32)
    gated = (gate_of(got_cot[:, features:]) * cotangent).astype(jnp.bfloat16)
    parts = expert_grad(
        all_normed,
        gather_x(gated),
        gate_weights,
        up_weights,
        down_weights,
    )
    summed = scatter_sum_x(parts)
    projection = jnp.mean(normed_bwd * summed, axis=-1, keepdims=True)
    grads = (cotangent + scale_bwd * (summed - normed_bwd * projection)).astype(jnp.bfloat16)
    output_grad = reorder(home_bwd.T, give_back(grads))
    return (output_act[None], output_grad[None])


def solution(mesh):
    fine = Mesh(mesh.devices.reshape(SIZES), AXES)
    rows = P(PP, EP, None)
    weights = P(PP, EP, None, None)
    return jax.shard_map(
        body,
        mesh=fine,
        in_specs=(rows,) * 7 + (weights,) * 3,
        out_specs=(rows, rows),
        check_vma=False,
    )
```

```python
import jax
import jax.numpy as jnp
from jax import lax
from jax.sharding import Mesh
from jax.sharding import PartitionSpec as P

AXES = ("y", "zh", "x", "zq", "zr", "c")
SIZES = (4, 2, 4, 2, 4, 2)
PP = ("y", "zh")
EP = ("x", "zq", "zr", "c")
Z16 = ("zh", "zq", "zr")
Z8 = ("zq", "zr")
EXPERTS = 8
DEPTH = 8
ROWS = EXPERTS * DEPTH
LANES = 128


epsilon = 1e-06


def normalize(activations):
    values = activations.astype(jnp.float32)
    rms_scale = lax.rsqrt(jnp.mean(values * values, axis=-1, keepdims=True) + epsilon)
    return (values * rms_scale, rms_scale)


def slot_matrix(routes):
    same = routes[:, None] == routes[None, :]
    order = jnp.arange(ROWS, dtype=jnp.int32)
    earlier = order[None, :] < order[:, None]
    rank = jnp.sum((same & earlier).astype(jnp.int32), axis=1)
    place = (routes % 2) * 4 + routes // 2
    slots = place * DEPTH + rank
    return (order[:, None] == slots[None, :]).astype(jnp.bfloat16)


def reorder(matrix, rows):
    return jnp.dot(matrix, rows, preferred_element_type=jnp.float32).astype(jnp.bfloat16)


def gate_lanes(gates):
    first = gates.astype(jnp.bfloat16)
    left = gates - first.astype(jnp.float32)
    second = left.astype(jnp.bfloat16)
    third = (left - second.astype(jnp.float32)).astype(jnp.bfloat16)
    three = jnp.stack([first, second, third], axis=1)
    return jnp.pad(three, ((0, 0), (0, LANES - 3)))


def gate_of(lanes):
    wide = lanes[:, :3].astype(jnp.float32)
    return (wide[:, 2:3] + wide[:, 1:2]) + wide[:, 0:1]


def rotated(x, axis, by):
    length = lax.axis_size(axis)
    return lax.ppermute(x, axis, [(i, (i + by) % length) for i in range(length)])


def gather_x(rows):
    return jnp.concatenate([rows] + [rotated(rows, "x", j) for j in (1, 2, 3)], axis=0)


def scatter_sum_x(parts):
    own = parts[:ROWS]
    sent = parts.astype(jnp.bfloat16)
    total = own.astype(jnp.bfloat16).astype(jnp.float32)
    for j in (1, 2, 3):
        total = total + rotated(sent[j * ROWS : (j + 1) * ROWS], "x", -j).astype(jnp.float32)
    return total


def nt(a, b):
    return lax.dot_general(a, b, (((1,), (1,)), ((), ())), preferred_element_type=jnp.float32)


def expert_out(rows, gate_up, down):
    gate_pre, up_pre = jnp.split(nt(rows, gate_up), 2, axis=1)
    hidden = (jax.nn.silu(gate_pre) * up_pre).astype(jnp.bfloat16)
    return jnp.dot(hidden, down, preferred_element_type=jnp.float32)


def expert_grad(rows, cotangents, gate_up, down):
    gate_pre, up_pre = jnp.split(nt(rows, gate_up), 2, axis=1)
    hidden_grad = nt(cotangents, down)
    sigmoid_val = jax.nn.sigmoid(gate_pre)
    gate_grad = (
        hidden_grad * up_pre * sigmoid_val * (1.0 + gate_pre * (1.0 - sigmoid_val))
    ).astype(jnp.bfloat16)
    up_grad = (hidden_grad * jax.nn.silu(gate_pre)).astype(jnp.bfloat16)
    return jnp.dot(
        jnp.concatenate([gate_grad, up_grad], axis=1), gate_up, preferred_element_type=jnp.float32
    )


def weights_along_x(w_gate, w_up, w_down):
    x, zr = lax.axis_index("x"), lax.axis_index("zr")
    stacked = jnp.stack([w_gate.T, w_up.T, w_down])
    units = stacked.shape[1] // 4
    pieces = stacked.reshape(3, 4, units, stacked.shape[2])

    def piece(index):
        return lax.dynamic_index_in_dim(pieces, index, axis=1, keepdims=False)

    return [piece(x)] + [rotated(piece((x + k) % 4), "x", k) for k in (1, 2, 3)]


def weights_along_z(pieces):
    x, zr = lax.axis_index("x"), lax.axis_index("zr")
    along_x = jnp.stack(pieces)
    blocks = [
        lax.dynamic_index_in_dim(along_x, (x - zr - m + 8) % 4, axis=0, keepdims=False)
        for m in range(4)
    ]
    return blocks[:1] + [rotated(blocks[m], "zr", m) for m in (1, 2, 3)]


def weights_of_chip(blocks):
    mine = jnp.concatenate(blocks, axis=1)
    other = lax.ppermute(mine, "c", [(0, 1), (1, 0)])
    both = jnp.concatenate([mine, other], axis=1)
    return both[:2].reshape(-1, both.shape[2]), both[2]


def body(
    carried, saved, grads_prev, routes_fwd, gates_fwd, routes_bwd, gates_bwd, w_gate, w_up, w_down
):
    high = lax.axis_index("zh")
    features = carried.shape[2]
    own_fwd, own_bwd = routes_fwd[0, :, 0], routes_bwd[0, :, 0]
    flat = jnp.stack(
        [own_fwd.astype(jnp.float32), gates_fwd[0, :, 0], own_bwd.astype(jnp.float32), gates_bwd[0, :, 0]]
    )
    is_high = high == 1
    along_y = jnp.where(is_high, carried[0], grads_prev[0])
    moves = []
    for y in range(4):
        moves.append((y * 2 + 1, ((y + 1) % 4) * 2 + 1))
        moves.append((y * 2, ((y + 3) % 4) * 2))
    along_y = lax.ppermute(along_y, PP, moves)
    flat = lax.ppermute(flat, "zh", [(0, 1), (1, 0)])
    mid_fwd, mid_bwd = flat[0].astype(jnp.int32), flat[2].astype(jnp.int32)
    fwd_rows = jnp.where(is_high, along_y, carried[0])
    cot_rows = jnp.where(is_high, grads_prev[0], along_y)

    blocks = weights_along_x(w_gate[0, 0], w_up[0, 0], w_down[0, 0])

    def dispatch(own, cross):
        both = jnp.concatenate(
            [jnp.where(is_high, cross, own), jnp.where(is_high, own, cross)], axis=0
        ).reshape(2 * EXPERTS, DEPTH, features + LANES)
        return lax.all_to_all(both, Z16, split_axis=0, concat_axis=0, tiled=True)

    def sides(got):
        got = got.reshape(2, ROWS, features + LANES)
        return jnp.where(is_high, got[1], got[0]), jnp.where(is_high, got[0], got[1])

    def give_back(rows):
        rows = rows.reshape(EXPERTS, DEPTH, features)
        return lax.all_to_all(rows, Z8, split_axis=0, concat_axis=0, tiled=True)

    home_bwd = slot_matrix(own_bwd)
    send_saved = jnp.pad(reorder(home_bwd, saved[0]), ((0, 0), (0, LANES)))
    send_fwd = reorder(
        slot_matrix(mid_fwd), jnp.concatenate([fwd_rows, gate_lanes(flat[1])], axis=1)
    )
    got_first = dispatch(send_saved, send_fwd)
    got_first, blocks = lax.optimization_barrier((got_first, blocks))
    got_saved, got_fwd = sides(got_first)
    blocks = weights_along_z(blocks)
    send_cot = reorder(
        slot_matrix(mid_bwd), jnp.concatenate([cot_rows, gate_lanes(flat[3])], axis=1)
    )
    send_cot, blocks = lax.optimization_barrier((send_cot, blocks))
    got_cot = dispatch(jnp.zeros_like(send_cot), send_cot)
    gate_up, down = weights_of_chip(blocks)

    section_input = got_fwd[:, :features]
    normed_fwd, _ = normalize(section_input)
    parts = expert_out(gather_x(normed_fwd.astype(jnp.bfloat16)), gate_up, down)
    normed_bwd, scale_bwd = normalize(got_saved[:, :features])
    all_normed = gather_x(normed_bwd.astype(jnp.bfloat16))
    mixed = scatter_sum_x(parts)
    mixed, all_normed, got_cot = lax.optimization_barrier((mixed, all_normed, got_cot))
    _, got_cot = sides(got_cot)
    cotangent = got_cot[:, :features].astype(jnp.float32)
    gated = (gate_of(got_cot[:, features:]) * cotangent).astype(jnp.bfloat16)
    mixed, gated = lax.optimization_barrier((mixed, gated))
    mixture = gate_of(got_fwd[:, features:]) * mixed
    acts = (section_input.astype(jnp.float32) + mixture).astype(jnp.bfloat16)
    got_acts = give_back(acts)
    parts = expert_grad(all_normed, gather_x(gated), gate_up, down)
    parts, got_acts = lax.optimization_barrier((parts, got_acts))
    summed = scatter_sum_x(parts)
    projection = jnp.mean(normed_bwd * summed, axis=-1, keepdims=True)
    grads = (cotangent + scale_bwd * (summed - normed_bwd * projection)).astype(jnp.bfloat16)
    output_grad = reorder(home_bwd.T, give_back(grads).reshape(ROWS, features))
    output_act = reorder(slot_matrix(own_fwd).T, got_acts.reshape(ROWS, features))
    return (output_act[None], output_grad[None])


def solution(mesh):
    fine = Mesh(mesh.devices.reshape(SIZES), AXES)
    rows = P(PP, EP, None)
    weights = P(PP, EP, None, None)
    return jax.shard_map(
        body,
        mesh=fine,
        in_specs=(rows,) * 7 + (weights,) * 3,
        out_specs=(rows, rows),
        check_vma=False,
    )
```

```python
import jax
import jax.numpy as jnp
from jax import lax
from jax.sharding import Mesh
from jax.sharding import PartitionSpec as P

AXES = ("y", "zh", "x", "zq", "zr", "c")
SIZES = (4, 2, 4, 2, 4, 2)
PP = ("y", "zh")
EP = ("x", "zq", "zr", "c")
Z16 = ("zh", "zq", "zr")
Z8 = ("zq", "zr")
EXPERTS = 8
DEPTH = 8
ROWS = EXPERTS * DEPTH
LANES = 128


epsilon = 1e-06


def normalize(activations):
    values = activations.astype(jnp.float32)
    rms_scale = lax.rsqrt(jnp.mean(values * values, axis=-1, keepdims=True) + epsilon)
    return (values * rms_scale, rms_scale)


def slot_matrix(routes):
    same = routes[:, None] == routes[None, :]
    order = jnp.arange(ROWS, dtype=jnp.int32)
    earlier = order[None, :] < order[:, None]
    rank = jnp.sum((same & earlier).astype(jnp.int32), axis=1)
    place = (routes % 2) * 4 + routes // 2
    slots = place * DEPTH + rank
    return (order[:, None] == slots[None, :]).astype(jnp.bfloat16)


def reorder(matrix, rows):
    return jnp.dot(matrix, rows, preferred_element_type=jnp.float32).astype(jnp.bfloat16)


def gate_lanes(gates):
    first = gates.astype(jnp.bfloat16)
    left = gates - first.astype(jnp.float32)
    second = left.astype(jnp.bfloat16)
    third = (left - second.astype(jnp.float32)).astype(jnp.bfloat16)
    three = jnp.stack([first, second, third], axis=1)
    return jnp.pad(three, ((0, 0), (0, LANES - 3)))


def gate_of(lanes):
    wide = lanes[:, :3].astype(jnp.float32)
    return (wide[:, 2:3] + wide[:, 1:2]) + wide[:, 0:1]


def rotated(x, axis, by):
    length = lax.axis_size(axis)
    return lax.ppermute(x, axis, [(i, (i + by) % length) for i in range(length)])


def around_x(rows):
    return [rows] + [rotated(rows, "x", j) for j in (1, 2, 3)]


def scatter_sum_x(first, second):
    def block(j):
        rows = slice(j * ROWS, (j + 1) * ROWS)
        return jnp.concatenate([first[rows], second[rows]], axis=0)

    total = block(0).astype(jnp.float32)
    for j in (2, 1, 3):
        total = total + rotated(block(j), "x", -j).astype(jnp.float32)
    return total


def nt(a, b):
    return lax.dot_general(a, b, (((1,), (1,)), ((), ())), preferred_element_type=jnp.float32)


def expert_out(rows, gate_up, down):
    gate_pre, up_pre = jnp.split(nt(rows, gate_up), 2, axis=1)
    hidden = (jax.nn.silu(gate_pre) * up_pre).astype(jnp.bfloat16)
    return jnp.dot(hidden, down, preferred_element_type=jnp.float32)


def expert_grad(rows, cotangents, gate_up, down):
    gate_pre, up_pre = jnp.split(nt(rows, gate_up), 2, axis=1)
    hidden_grad = nt(cotangents, down)
    sigmoid_val = jax.nn.sigmoid(gate_pre)
    gate_grad = (
        hidden_grad * up_pre * sigmoid_val * (1.0 + gate_pre * (1.0 - sigmoid_val))
    ).astype(jnp.bfloat16)
    up_grad = (hidden_grad * jax.nn.silu(gate_pre)).astype(jnp.bfloat16)
    return jnp.dot(
        jnp.concatenate([gate_grad, up_grad], axis=1), gate_up, preferred_element_type=jnp.float32
    )


def weights_along_x(w_gate, w_up, w_down):
    x, zr = lax.axis_index("x"), lax.axis_index("zr")
    stacked = jnp.stack([w_gate.T, w_up.T, w_down])
    units = stacked.shape[1] // 4
    pieces = stacked.reshape(3, 4, units, stacked.shape[2])

    def piece(index):
        return lax.dynamic_index_in_dim(pieces, index, axis=1, keepdims=False)

    along_x = jnp.stack(
        [piece(x)] + [rotated(piece((x + k) % 4), "x", k) for k in (1, 2, 3)]
    )
    return [
        lax.dynamic_index_in_dim(along_x, (x - zr - m + 8) % 4, axis=0, keepdims=False)
        for m in range(4)
    ]


def weights_along_z(blocks):
    return blocks[:1] + [rotated(blocks[m], "zr", m) for m in (1, 2, 3)]


def both_cores(blocks):
    mine = jnp.concatenate(blocks, axis=1)
    return [mine, lax.ppermute(mine, "c", [(0, 1), (1, 0)])]


def body(
    carried, saved, grads_prev, routes_fwd, gates_fwd, routes_bwd, gates_bwd, w_gate, w_up, w_down
):
    high = lax.axis_index("zh")
    features = carried.shape[2]
    own_fwd, own_bwd = routes_fwd[0, :, 0], routes_bwd[0, :, 0]
    flat = jnp.stack(
        [own_fwd.astype(jnp.float32), gates_fwd[0, :, 0], own_bwd.astype(jnp.float32), gates_bwd[0, :, 0]]
    )
    is_high = high == 1
    along_y = jnp.where(is_high, carried[0], grads_prev[0])
    moves = []
    for y in range(4):
        moves.append((y * 2 + 1, ((y + 1) % 4) * 2 + 1))
        moves.append((y * 2, ((y + 3) % 4) * 2))
    along_y = lax.ppermute(along_y, PP, moves)
    flat = lax.ppermute(flat, "zh", [(0, 1), (1, 0)])
    mid_fwd, mid_bwd = flat[0].astype(jnp.int32), flat[2].astype(jnp.int32)
    fwd_rows = jnp.where(is_high, along_y, carried[0])
    cot_rows = jnp.where(is_high, grads_prev[0], along_y)

    blocks = weights_along_x(w_gate[0, 0], w_up[0, 0], w_down[0, 0])

    def dispatch(own, cross):
        both = jnp.concatenate(
            [jnp.where(is_high, cross, own), jnp.where(is_high, own, cross)], axis=0
        ).reshape(2 * EXPERTS, DEPTH, features + LANES)
        return lax.all_to_all(both, Z16, split_axis=0, concat_axis=0, tiled=True)

    def sides(got):
        got = got.reshape(2, ROWS, features + LANES)
        return jnp.where(is_high, got[1], got[0]), jnp.where(is_high, got[0], got[1])

    home_bwd = slot_matrix(own_bwd)
    send_saved = jnp.pad(reorder(home_bwd, saved[0]), ((0, 0), (0, LANES)))
    send_fwd = reorder(
        slot_matrix(mid_fwd), jnp.concatenate([fwd_rows, gate_lanes(flat[1])], axis=1)
    )
    got_first = dispatch(send_saved, send_fwd)
    got_first, blocks = lax.optimization_barrier((got_first, blocks))
    got_saved, got_fwd = sides(got_first)
    section_input = got_fwd[:, :features]
    normed_fwd, _ = normalize(section_input)
    normed_bwd, scale_bwd = normalize(got_saved[:, :features])
    rows = jnp.concatenate([normed_fwd, normed_bwd], axis=0).astype(jnp.bfloat16)
    blocks = weights_along_z(blocks)
    rows, blocks[1] = lax.optimization_barrier((rows, blocks[1]))
    gathered = around_x(rows)
    send_cot = reorder(
        slot_matrix(mid_bwd), jnp.concatenate([cot_rows, gate_lanes(flat[3])], axis=1)
    )
    got_cot = dispatch(jnp.zeros_like(send_cot), send_cot)
    gathered, got_cot = lax.optimization_barrier((gathered, got_cot))
    _, got_cot = sides(got_cot)
    cotangent = got_cot[:, :features].astype(jnp.float32)
    gated = (gate_of(got_cot[:, features:]) * cotangent).astype(jnp.bfloat16)
    all_gated = around_x(gated)
    all_gated, late = lax.optimization_barrier((all_gated, blocks[2:]))
    held = both_cores(blocks[:2]) + both_cores(late)
    gate_up = jnp.concatenate([part[:2] for part in held], axis=1).reshape(-1, features)
    down = jnp.concatenate([part[2] for part in held], axis=0)

    all_fwd = jnp.concatenate([rows[:ROWS] for rows in gathered], axis=0)
    all_bwd = jnp.concatenate([rows[ROWS:] for rows in gathered], axis=0)
    parts_fwd = expert_out(all_fwd, gate_up, down).astype(jnp.bfloat16)
    parts_bwd = expert_grad(all_bwd, jnp.concatenate(all_gated, axis=0), gate_up, down).astype(
        jnp.bfloat16
    )
    summed = scatter_sum_x(parts_fwd, parts_bwd)
    summed_fwd, summed_bwd = summed[:ROWS], summed[ROWS:]
    mixture = gate_of(got_fwd[:, features:]) * summed_fwd
    acts = (section_input.astype(jnp.float32) + mixture).astype(jnp.bfloat16)
    projection = jnp.mean(normed_bwd * summed_bwd, axis=-1, keepdims=True)
    grads = (cotangent + scale_bwd * (summed_bwd - normed_bwd * projection)).astype(jnp.bfloat16)
    back = jnp.concatenate(
        [rows.reshape(EXPERTS, DEPTH, features) for rows in (acts, grads)], axis=1
    )
    back = lax.all_to_all(back, Z8, split_axis=0, concat_axis=0, tiled=True)
    output_act = reorder(slot_matrix(own_fwd).T, back[:, :DEPTH].reshape(ROWS, features))
    output_grad = reorder(home_bwd.T, back[:, DEPTH:].reshape(ROWS, features))
    return (output_act[None], output_grad[None])


def solution(mesh):
    fine = Mesh(mesh.devices.reshape(SIZES), AXES)
    rows = P(PP, EP, None)
    weights = P(PP, EP, None, None)
    return jax.shard_map(
        body,
        mesh=fine,
        in_specs=(rows,) * 7 + (weights,) * 3,
        out_specs=(rows, rows),
        check_vma=False,
    )
```

```python
import jax
import jax.numpy as jnp
from jax import lax
from jax.sharding import Mesh
from jax.sharding import PartitionSpec as P

AXES = ("y", "zh", "x", "zq", "zr", "c")
SIZES = (4, 2, 4, 2, 4, 2)
PP = ("y", "zh")
EP = ("x", "zq", "zr", "c")
Z16 = ("zh", "zq", "zr")
Z8 = ("zq", "zr")
EXPERTS = 8
DEPTH = 8
ROWS = EXPERTS * DEPTH
LANES = 128


epsilon = 1e-06


def normalize(activations):
    values = activations.astype(jnp.float32)
    rms_scale = lax.rsqrt(jnp.mean(values * values, axis=-1, keepdims=True) + epsilon)
    return (values * rms_scale, rms_scale)


def slot_matrix(routes):
    same = routes[:, None] == routes[None, :]
    order = jnp.arange(ROWS, dtype=jnp.int32)
    earlier = order[None, :] < order[:, None]
    rank = jnp.sum((same & earlier).astype(jnp.int32), axis=1)
    place = (routes % 2) * 4 + routes // 2
    slots = place * DEPTH + rank
    return (order[:, None] == slots[None, :]).astype(jnp.bfloat16)


def reorder(matrix, rows):
    return jnp.dot(matrix, rows, preferred_element_type=jnp.float32).astype(jnp.bfloat16)


def gate_lanes(gates):
    first = gates.astype(jnp.bfloat16)
    left = gates - first.astype(jnp.float32)
    second = left.astype(jnp.bfloat16)
    third = (left - second.astype(jnp.float32)).astype(jnp.bfloat16)
    three = jnp.stack([first, second, third], axis=1)
    return jnp.pad(three, ((0, 0), (0, LANES - 3)))


def gate_of(lanes):
    wide = lanes[:, :3].astype(jnp.float32)
    return (wide[:, 2:3] + wide[:, 1:2]) + wide[:, 0:1]


def rotated(x, axis, by):
    length = lax.axis_size(axis)
    return lax.ppermute(x, axis, [(i, (i + by) % length) for i in range(length)])


def around_x(rows):
    return [rows] + [rotated(rows, "x", j) for j in (1, 2, 3)]


def scatter_sum_x(parts):
    total = parts[:ROWS].astype(jnp.float32)
    for j in (2, 1, 3):
        total = total + rotated(parts[j * ROWS : (j + 1) * ROWS], "x", -j).astype(jnp.float32)
    return total


def nt(a, b):
    return lax.dot_general(a, b, (((1,), (1,)), ((), ())), preferred_element_type=jnp.float32)


def expert_out(rows, gate_up, down):
    gate_pre, up_pre = jnp.split(nt(rows, gate_up), 2, axis=1)
    hidden = (jax.nn.silu(gate_pre) * up_pre).astype(jnp.bfloat16)
    return jnp.dot(hidden, down, preferred_element_type=jnp.float32)


def expert_grad(rows, cotangents, gate_up, down):
    gate_pre, up_pre = jnp.split(nt(rows, gate_up), 2, axis=1)
    hidden_grad = nt(cotangents, down)
    sigmoid_val = jax.nn.sigmoid(gate_pre)
    gate_grad = (
        hidden_grad * up_pre * sigmoid_val * (1.0 + gate_pre * (1.0 - sigmoid_val))
    ).astype(jnp.bfloat16)
    up_grad = (hidden_grad * jax.nn.silu(gate_pre)).astype(jnp.bfloat16)
    return jnp.dot(
        jnp.concatenate([gate_grad, up_grad], axis=1), gate_up, preferred_element_type=jnp.float32
    )


def weights_along_x(w_gate, w_up, w_down):
    x, zr = lax.axis_index("x"), lax.axis_index("zr")
    stacked = jnp.stack([w_gate.T, w_up.T, w_down])
    units = stacked.shape[1] // 4
    pieces = stacked.reshape(3, 4, units, stacked.shape[2])

    def piece(index):
        return lax.dynamic_index_in_dim(pieces, index, axis=1, keepdims=False)

    along_x = jnp.stack(
        [piece(x)] + [rotated(piece((x + k) % 4), "x", k) for k in (1, 2, 3)]
    )
    return [
        lax.dynamic_index_in_dim(along_x, (x - zr - m + 8) % 4, axis=0, keepdims=False)
        for m in range(4)
    ]


def weights_along_z(blocks):
    return blocks[:1] + [rotated(blocks[m], "zr", m) for m in (1, 2, 3)]


def both_cores(blocks):
    mine = jnp.concatenate(blocks, axis=1)
    return [mine, lax.ppermute(mine, "c", [(0, 1), (1, 0)])]


def body(
    carried, saved, grads_prev, routes_fwd, gates_fwd, routes_bwd, gates_bwd, w_gate, w_up, w_down
):
    high = lax.axis_index("zh")
    features = carried.shape[2]
    own_fwd, own_bwd = routes_fwd[0, :, 0], routes_bwd[0, :, 0]
    flat = jnp.stack(
        [own_fwd.astype(jnp.float32), gates_fwd[0, :, 0], own_bwd.astype(jnp.float32), gates_bwd[0, :, 0]]
    )
    is_high = high == 1
    along_y = jnp.where(is_high, carried[0], grads_prev[0])
    moves = []
    for y in range(4):
        moves.append((y * 2 + 1, ((y + 1) % 4) * 2 + 1))
        moves.append((y * 2, ((y + 3) % 4) * 2))
    along_y = lax.ppermute(along_y, PP, moves)
    flat = lax.ppermute(flat, "zh", [(0, 1), (1, 0)])
    mid_fwd, mid_bwd = flat[0].astype(jnp.int32), flat[2].astype(jnp.int32)
    fwd_rows = jnp.where(is_high, along_y, carried[0])
    cot_rows = jnp.where(is_high, grads_prev[0], along_y)

    blocks = weights_along_x(w_gate[0, 0], w_up[0, 0], w_down[0, 0])

    def dispatch(own, cross):
        both = jnp.concatenate(
            [jnp.where(is_high, cross, own), jnp.where(is_high, own, cross)], axis=0
        ).reshape(2 * EXPERTS, DEPTH, features + LANES)
        return lax.all_to_all(both, Z16, split_axis=0, concat_axis=0, tiled=True)

    def sides(got):
        got = got.reshape(2, ROWS, features + LANES)
        return jnp.where(is_high, got[1], got[0]), jnp.where(is_high, got[0], got[1])

    home_bwd = slot_matrix(own_bwd)
    send_saved = jnp.pad(reorder(home_bwd, saved[0]), ((0, 0), (0, LANES)))
    send_fwd = reorder(
        slot_matrix(mid_fwd), jnp.concatenate([fwd_rows, gate_lanes(flat[1])], axis=1)
    )
    got_first = dispatch(send_saved, send_fwd)
    got_first, blocks = lax.optimization_barrier((got_first, blocks))
    got_saved, got_fwd = sides(got_first)
    section_input = got_fwd[:, :features]
    normed_fwd, _ = normalize(section_input)
    normed_bwd, scale_bwd = normalize(got_saved[:, :features])
    rows = jnp.concatenate([normed_fwd, normed_bwd], axis=0).astype(jnp.bfloat16)
    rows, blocks = lax.optimization_barrier((rows, blocks))
    blocks = weights_along_z(blocks)
    gathered = around_x(rows)
    send_cot = reorder(
        slot_matrix(mid_bwd), jnp.concatenate([cot_rows, gate_lanes(flat[3])], axis=1)
    )
    got_cot = dispatch(jnp.zeros_like(send_cot), send_cot)
    gathered, got_cot = lax.optimization_barrier((gathered, got_cot))
    _, got_cot = sides(got_cot)
    cotangent = got_cot[:, :features].astype(jnp.float32)
    gated = (gate_of(got_cot[:, features:]) * cotangent).astype(jnp.bfloat16)
    all_gated = around_x(gated)
    all_gated, late = lax.optimization_barrier((all_gated, blocks[2:]))
    held = both_cores(blocks[:2]) + both_cores(late)
    gate_up = jnp.concatenate([part[:2] for part in held], axis=1).reshape(-1, features)
    down = jnp.concatenate([part[2] for part in held], axis=0)

    all_fwd = jnp.concatenate([rows[:ROWS] for rows in gathered], axis=0)
    all_bwd = jnp.concatenate([rows[ROWS:] for rows in gathered], axis=0)
    parts_fwd = expert_out(all_fwd, gate_up, down).astype(jnp.bfloat16)
    parts_bwd = expert_grad(all_bwd, jnp.concatenate(all_gated, axis=0), gate_up, down).astype(
        jnp.bfloat16
    )
    def give_back(rows):
        rows = rows.reshape(EXPERTS, DEPTH, features)
        got = lax.all_to_all(rows, Z8, split_axis=0, concat_axis=0, tiled=True)
        return got.reshape(ROWS, features)

    summed = scatter_sum_x(parts_bwd)
    projection = jnp.mean(normed_bwd * summed, axis=-1, keepdims=True)
    grads = (cotangent + scale_bwd * (summed - normed_bwd * projection)).astype(jnp.bfloat16)
    output_grad = reorder(home_bwd.T, give_back(grads))

    mixture = gate_of(got_fwd[:, features:]) * scatter_sum_x(parts_fwd)
    acts = (section_input.astype(jnp.float32) + mixture).astype(jnp.bfloat16)
    output_act = reorder(slot_matrix(own_fwd).T, give_back(acts))
    return (output_act[None], output_grad[None])


def solution(mesh):
    fine = Mesh(mesh.devices.reshape(SIZES), AXES)
    rows = P(PP, EP, None)
    weights = P(PP, EP, None, None)
    return jax.shard_map(
        body,
        mesh=fine,
        in_specs=(rows,) * 7 + (weights,) * 3,
        out_specs=(rows, rows),
        check_vma=False,
    )
```

```python
import jax
import jax.numpy as jnp
from jax import lax
from jax.sharding import Mesh
from jax.sharding import PartitionSpec as P

AXES = ("y", "zh", "x", "zq", "zr", "c")
SIZES = (4, 2, 4, 2, 4, 2)
PP = ("y", "zh")
EP = ("x", "zq", "zr", "c")
Z16 = ("zh", "zq", "zr")
Z8 = ("zq", "zr")
EXPERTS = 8
DEPTH = 8
ROWS = EXPERTS * DEPTH
LANES = 128


epsilon = 1e-06


def normalize(activations):
    values = activations.astype(jnp.float32)
    rms_scale = lax.rsqrt(jnp.mean(values * values, axis=-1, keepdims=True) + epsilon)
    return (values * rms_scale, rms_scale)


def slot_matrix(routes):
    same = routes[:, None] == routes[None, :]
    order = jnp.arange(ROWS, dtype=jnp.int32)
    earlier = order[None, :] < order[:, None]
    rank = jnp.sum((same & earlier).astype(jnp.int32), axis=1)
    place = (routes % 2) * 4 + routes // 2
    slots = place * DEPTH + rank
    return (order[:, None] == slots[None, :]).astype(jnp.bfloat16)


def reorder(matrix, rows):
    return jnp.dot(matrix, rows, preferred_element_type=jnp.float32).astype(jnp.bfloat16)


def gate_lanes(gates):
    first = gates.astype(jnp.bfloat16)
    left = gates - first.astype(jnp.float32)
    second = left.astype(jnp.bfloat16)
    third = (left - second.astype(jnp.float32)).astype(jnp.bfloat16)
    three = jnp.stack([first, second, third], axis=1)
    return jnp.pad(three, ((0, 0), (0, LANES - 3)))


def gate_of(lanes):
    wide = lanes[:, :3].astype(jnp.float32)
    return (wide[:, 2:3] + wide[:, 1:2]) + wide[:, 0:1]


def rotated(x, axis, by):
    length = lax.axis_size(axis)
    return lax.ppermute(x, axis, [(i, (i + by) % length) for i in range(length)])


def around_x(rows):
    return [rows] + [rotated(rows, "x", j) for j in (1, 2, 3)]


def scatter_sum_x(parts):
    total = parts[:ROWS].astype(jnp.float32)
    for j in (2, 1, 3):
        total = total + rotated(parts[j * ROWS : (j + 1) * ROWS], "x", -j).astype(jnp.float32)
    return total


def nt(a, b):
    return lax.dot_general(a, b, (((1,), (1,)), ((), ())), preferred_element_type=jnp.float32)


def expert_out(rows, gate_up, down):
    gate_pre, up_pre = jnp.split(nt(rows, gate_up), 2, axis=1)
    hidden = (jax.nn.silu(gate_pre) * up_pre).astype(jnp.bfloat16)
    return jnp.dot(hidden, down, preferred_element_type=jnp.float32)


def expert_grad(rows, cotangents, gate_up, down):
    gate_pre, up_pre = jnp.split(nt(rows, gate_up), 2, axis=1)
    hidden_grad = nt(cotangents, down)
    sigmoid_val = jax.nn.sigmoid(gate_pre)
    gate_grad = (
        hidden_grad * up_pre * sigmoid_val * (1.0 + gate_pre * (1.0 - sigmoid_val))
    ).astype(jnp.bfloat16)
    up_grad = (hidden_grad * jax.nn.silu(gate_pre)).astype(jnp.bfloat16)
    return jnp.dot(
        jnp.concatenate([gate_grad, up_grad], axis=1), gate_up, preferred_element_type=jnp.float32
    )


def weights_along_x(w_gate, w_up, w_down):
    x, zr = lax.axis_index("x"), lax.axis_index("zr")
    stacked = jnp.stack([w_gate.T, w_up.T, w_down])
    units = stacked.shape[1] // 4
    pieces = stacked.reshape(3, 4, units, stacked.shape[2])

    def piece(index):
        return lax.dynamic_index_in_dim(pieces, index, axis=1, keepdims=False)

    along_x = jnp.stack(
        [piece(x)] + [rotated(piece((x + k) % 4), "x", k) for k in (1, 2, 3)]
    )
    return [
        lax.dynamic_index_in_dim(along_x, (x - zr - m + 8) % 4, axis=0, keepdims=False)
        for m in range(4)
    ]


def weights_along_z(blocks):
    return blocks[:1] + [rotated(blocks[m], "zr", m) for m in (1, 2, 3)]


def both_cores(blocks):
    mine = jnp.concatenate(blocks, axis=1)
    return [mine, lax.ppermute(mine, "c", [(0, 1), (1, 0)])]


def body(
    carried, saved, grads_prev, routes_fwd, gates_fwd, routes_bwd, gates_bwd, w_gate, w_up, w_down
):
    high = lax.axis_index("zh")
    features = carried.shape[2]
    own_fwd, own_bwd = routes_fwd[0, :, 0], routes_bwd[0, :, 0]
    flat = jnp.stack(
        [own_fwd.astype(jnp.float32), gates_fwd[0, :, 0], own_bwd.astype(jnp.float32), gates_bwd[0, :, 0]]
    )
    is_high = high == 1
    along_y = jnp.where(is_high, carried[0], grads_prev[0])
    moves = []
    for y in range(4):
        moves.append((y * 2 + 1, ((y + 1) % 4) * 2 + 1))
        moves.append((y * 2, ((y + 3) % 4) * 2))
    along_y = lax.ppermute(along_y, PP, moves)
    flat = lax.ppermute(flat, "zh", [(0, 1), (1, 0)])
    mid_fwd, mid_bwd = flat[0].astype(jnp.int32), flat[2].astype(jnp.int32)
    fwd_rows = jnp.where(is_high, along_y, carried[0])
    cot_rows = jnp.where(is_high, grads_prev[0], along_y)

    blocks = weights_along_x(w_gate[0, 0], w_up[0, 0], w_down[0, 0])

    def dispatch(own, cross):
        both = jnp.concatenate(
            [jnp.where(is_high, cross, own), jnp.where(is_high, own, cross)], axis=0
        ).reshape(2 * EXPERTS, DEPTH, features + LANES)
        return lax.all_to_all(both, Z16, split_axis=0, concat_axis=0, tiled=True)

    def sides(got):
        got = got.reshape(2, ROWS, features + LANES)
        return jnp.where(is_high, got[1], got[0]), jnp.where(is_high, got[0], got[1])

    home_bwd = slot_matrix(own_bwd)
    send_saved = jnp.pad(reorder(home_bwd, saved[0]), ((0, 0), (0, LANES)))
    send_fwd = reorder(
        slot_matrix(mid_fwd), jnp.concatenate([fwd_rows, gate_lanes(flat[1])], axis=1)
    )
    got_first = dispatch(send_saved, send_fwd)
    got_first, blocks = lax.optimization_barrier((got_first, blocks))
    got_saved, got_fwd = sides(got_first)
    section_input = got_fwd[:, :features]
    normed_fwd, _ = normalize(section_input)
    normed_bwd, scale_bwd = normalize(got_saved[:, :features])
    rows = jnp.concatenate([normed_fwd, normed_bwd], axis=0).astype(jnp.bfloat16)
    rows, blocks = lax.optimization_barrier((rows, blocks))
    blocks = weights_along_z(blocks)
    gathered = lax.all_gather(rows, "x")
    send_cot = reorder(
        slot_matrix(mid_bwd), jnp.concatenate([cot_rows, gate_lanes(flat[3])], axis=1)
    )
    got_cot = dispatch(jnp.zeros_like(send_cot), send_cot)
    gathered, got_cot = lax.optimization_barrier((gathered, got_cot))
    x = lax.axis_index("x")
    gathered = [
        lax.dynamic_index_in_dim(gathered, (x - j + 4) % 4, axis=0, keepdims=False) for j in range(4)
    ]
    _, got_cot = sides(got_cot)
    cotangent = got_cot[:, :features].astype(jnp.float32)
    gated = (gate_of(got_cot[:, features:]) * cotangent).astype(jnp.bfloat16)
    all_gated = around_x(gated)
    all_gated, late = lax.optimization_barrier((all_gated, blocks[2:]))
    held = both_cores(blocks[:2]) + both_cores(late)
    gate_up = jnp.concatenate([part[:2] for part in held], axis=1).reshape(-1, features)
    down = jnp.concatenate([part[2] for part in held], axis=0)

    all_fwd = jnp.concatenate([rows[:ROWS] for rows in gathered], axis=0)
    all_bwd = jnp.concatenate([rows[ROWS:] for rows in gathered], axis=0)
    parts_fwd = expert_out(all_fwd, gate_up, down).astype(jnp.bfloat16)
    parts_bwd = expert_grad(all_bwd, jnp.concatenate(all_gated, axis=0), gate_up, down).astype(
        jnp.bfloat16
    )
    def give_back(rows):
        rows = rows.reshape(EXPERTS, DEPTH, features)
        got = lax.all_to_all(rows, Z8, split_axis=0, concat_axis=0, tiled=True)
        return got.reshape(ROWS, features)

    summed = scatter_sum_x(parts_bwd)
    projection = jnp.mean(normed_bwd * summed, axis=-1, keepdims=True)
    grads = (cotangent + scale_bwd * (summed - normed_bwd * projection)).astype(jnp.bfloat16)
    output_grad = reorder(home_bwd.T, give_back(grads))

    mixture = gate_of(got_fwd[:, features:]) * scatter_sum_x(parts_fwd)
    acts = (section_input.astype(jnp.float32) + mixture).astype(jnp.bfloat16)
    output_act = reorder(slot_matrix(own_fwd).T, give_back(acts))
    return (output_act[None], output_grad[None])


def solution(mesh):
    fine = Mesh(mesh.devices.reshape(SIZES), AXES)
    rows = P(PP, EP, None)
    weights = P(PP, EP, None, None)
    return jax.shard_map(
        body,
        mesh=fine,
        in_specs=(rows,) * 7 + (weights,) * 3,
        out_specs=(rows, rows),
        check_vma=False,
    )
```
